32 devices in a mesh: parts: 2 (over y), span: 4 (over x, core), seq: 4 (over z).
Axes of the slice: x: 2, y: 2, z: 4, core: 2. Of those that a mesh axis runs over, the one named last changes fastest.
Arguments:
- q_in: bfloat16 [8, 1024, 4096], P(('parts', 'span'), 'seq'), parts along dimension 0, may hold values from -9 to 9
- k_in: bfloat16 [8, 1024, 4096], P(('parts', 'span'), 'seq'), parts along dimension 0, may hold values from -9 to 9
- v_in: bfloat16 [8, 1024, 4096], P(('parts', 'span'), 'seq'), parts along dimension 0, may hold values from -18 to 18
- timesteps: int32 [8], P('parts'), parts along dimension 0, may hold values from 0 to 31
- gate_table: float32 [32, 4096], replicated, may hold values from 0.1 to 1.9
Outputs:
- gated_out: bfloat16 [8, 1024, 4096], P(('parts', 'span'), 'seq'), parts along dimension 0
The draws below stay inside these ranges and needn't reach their ends.
There are 2 independent parts, one for each index of `parts`. The reference program is written for one: setup_inputs(seed, part) draws one part's arguments, and reference() takes and returns one part's arrays. A program takes and returns all parts, laid end to end along the dimension named above; an argument that names none is the same for every part. Nothing has to cross between parts.
All inputs are finite; a program needn't handle non-finite values.
Results may differ from the reference program's by a relative error of at most 0.0053.
Values may be sent and summed in bfloat16 or wider, within the bound.
A program may use at most 128 MiB of HBM per device.

```python
import jax
import jax.numpy as jnp
from jax import lax

H = 32
HD = 128
SPAN_LEN = 1024
STEPS = 32
SPANS = 4


def base_field(key):
    shape = (SPANS, SPAN_LEN, H * HD)
    field = jnp.clip(jax.random.normal(key, shape, jnp.float32) * 1.41, -8.5, 8.5)
    return field


def draw_q_in(key, part):
    field = base_field(jax.random.fold_in(key, 1))
    return field.astype(jnp.bfloat16)


def draw_k_in(key, part):
    field = base_field(jax.random.fold_in(key, 2))
    return field.astype(jnp.bfloat16)


def set_ends(array, stream_key, low, high):
    spot = [jax.random.randint(jax.random.fold_in(stream_key, axis), (), 0, length) for axis, length in enumerate(array.shape)]
    widest = array.shape.index(max(array.shape))
    next_to = spot[:widest] + [(spot[widest] + 1) % array.shape[widest]] + spot[widest + 1:]
    return array.at[tuple(spot)].set(low).at[tuple(next_to)].set(high)


def block_levels(own_key, dims, pieces, smallest, high):
    level = 1.0
    for position, shards_of in pieces:
        steps = jax.random.uniform(jax.random.fold_in(jax.random.fold_in(own_key, 6), position), (shards_of,), jnp.float32, smallest / len(pieces), high / len(pieces))
        level = level * jnp.repeat(jnp.exp(steps), dims[position] // shards_of).reshape((-1,) + (1,) * (len(dims) - 1 - position))
    return level


def centred(rng, shape, width, limit, shards=(), kind=jnp.bfloat16):
    level = block_levels(rng, shape, shards, -0.22, 0.18) if shards else 1.0
    entries = jax.random.normal(rng, shape, jnp.float32) * width * level
    return jnp.minimum(jnp.maximum(entries, -limit), limit).astype(kind)


def setup_inputs(seed: int = 0, part: int = 0) -> dict:
    seeds = jax.random.split(jax.random.key(seed), 6)
    part_splits = jax.random.split(jax.random.fold_in(seeds[5], part), 6)
    q_in = draw_q_in(jax.random.fold_in(jax.random.fold_in(seeds[5], part), 71), part)
    k_in = draw_k_in(jax.random.fold_in(jax.random.fold_in(seeds[5], part), 71), part)
    v_in = centred(part_splits[2], (SPANS, SPAN_LEN, H * HD), 3.0, 18.0, ((0, 4), (1, 4)))
    timesteps = set_ends(jax.random.randint(part_splits[3], (SPANS,), 0, STEPS), jax.random.fold_in(part_splits[3], 1), 0, STEPS - 1).astype(jnp.int32)
    gate_table = jnp.clip(1.0 + 0.18 * jax.random.normal(seeds[4], (STEPS, H * HD), jnp.float32), 0.1, 1.9)
    return {"q_in": q_in, "k_in": k_in, "v_in": v_in, "timesteps": timesteps, "gate_table": gate_table}


def reference(q_in, k_in, v_in, timesteps, gate_table):
    scale = HD ** -0.5
    query_heads = q_in.reshape(SPANS, SPAN_LEN, H, HD).transpose(2, 0, 1, 3)
    key_heads = k_in.reshape(SPANS * SPAN_LEN, H, HD).transpose(1, 0, 2)
    value_heads = v_in.reshape(SPANS * SPAN_LEN, H, HD).transpose(1, 0, 2)
    key_span = (jnp.arange(SPANS * SPAN_LEN) // SPAN_LEN).astype(jnp.int32)

    def one_head(packed):
        queries, keys, values = packed

        def one_span(index):
            query = queries[index]
            scores = jnp.dot(query, keys.T, preferred_element_type=jnp.float32) * scale
            visible = key_span <= index
            scores = jnp.where(visible[None, :], scores, -jnp.inf)
            rowmax = jnp.max(scores, axis=-1, keepdims=True)
            expo = jnp.exp(scores - rowmax)
            total = jnp.sum(expo, axis=-1, keepdims=True)
            weights = expo.astype(jnp.bfloat16)
            mixed = jnp.dot(weights, values, preferred_element_type=jnp.float32) / total
            return mixed.astype(jnp.bfloat16)

        return lax.map(one_span, jnp.arange(SPANS).astype(jnp.int32))

    attn = lax.map(one_head, (query_heads, key_heads, value_heads))
    attn = attn.transpose(1, 2, 0, 3).reshape(SPANS, SPAN_LEN, H * HD)
    gates = gate_table[timesteps]
    return (attn.astype(jnp.float32) * gates[:, None, :]).astype(jnp.bfloat16)
```

```python
import functools
import math

import jax
import jax.numpy as jnp
from jax import lax
from jax.experimental import pallas as pl
from jax.experimental.pallas import tpu as pltpu
from jax.sharding import PartitionSpec as P

HD = 128
AHEAD = 3
MESH = pl.DeviceIdType.MESH


def kernel(
    n, spans, q_in, k_in, v_in, gate, out, q_all, k_all, v_all, o_all,
    send_z, recv_z, send_x, send_c, recv_s, send_o, recv_o,
):
    heads, length, _ = q_all.shape
    rows = length // n
    cores = 2 if spans % 2 == 0 else 1
    chips = spans // cores
    z = lax.axis_index("seq")
    span = lax.axis_index("span")
    chip = span // cores
    core = lax.rem(span, cores)
    sibling = chip * cores + (cores - 1 - core)
    coef = HD ** (-0.5) * math.log2(math.e)

    barrier = pltpu.get_barrier_semaphore()

    def greet_seq(step, carry):
        pl.semaphore_signal(
            barrier, inc=1, device_id={"seq": lax.rem(z + step, n)}, device_id_type=MESH
        )
        return carry

    def greet_span(step, carry):
        other = lax.rem(chip + step, chips) * cores + core
        pl.semaphore_signal(barrier, inc=1, device_id={"span": other}, device_id_type=MESH)
        return carry

    lax.fori_loop(1, n, greet_seq, 0)
    lax.fori_loop(1, chips, greet_span, 0)
    if cores == 2:
        pl.semaphore_signal(barrier, inc=1, device_id={"span": sibling}, device_id_type=MESH)
    pl.semaphore_wait(barrier, (n - 1) + (chips - 1) + (cores - 1))

    def token_rows(index):
        return pl.ds(pl.multiple_of(index * rows, rows), rows)

    def head_columns(owner, head):
        return pl.ds(pl.multiple_of((owner * heads + head) * HD, HD), HD)

    sources = (k_in, v_in, q_in)

    def landing(which, head, piece):
        if which == 2:
            return q_all.at[head, token_rows(piece), :]
        return (k_all, v_all)[which].at[span, head, token_rows(piece), :]

    def own_piece(which, head):
        return pltpu.make_async_copy(
            sources[which].at[:, head_columns(z, head)],
            landing(which, head, z),
            recv_z.at[which, head, z],
        )

    def seq_send(which, head, peer):
        return pltpu.make_async_remote_copy(
            src_ref=sources[which].at[:, head_columns(peer, head)],
            dst_ref=landing(which, head, z),
            send_sem=send_z.at[which, head, peer],
            recv_sem=recv_z.at[which, head, z],
            device_id={"seq": peer},
            device_id_type=MESH,
        )

    def seq_arrival(which, head, peer):
        return pltpu.make_async_remote_copy(
            src_ref=sources[which].at[:, head_columns(peer, head)],
            dst_ref=landing(which, head, peer),
            send_sem=send_z.at[which, head, peer],
            recv_sem=recv_z.at[which, head, peer],
            device_id={"seq": peer},
            device_id_type=MESH,
        )

    def span_copy(which, head, origin, target, send_sem):
        block = (k_all, v_all)[which].at[origin, head]
        return pltpu.make_async_remote_copy(
            src_ref=block,
            dst_ref=block,
            send_sem=send_sem,
            recv_sem=recv_s.at[which, head, origin],
            device_id={"span": target},
            device_id_type=MESH,
        )

    def chip_send(which, head, other_chip):
        return span_copy(
            which, head, span, other_chip * cores + core, send_x.at[which, head, other_chip]
        )

    def sibling_send(which, head, origin):
        return span_copy(which, head, origin, sibling, send_c.at[which, head, origin])

    def result_send(head, peer):
        return pltpu.make_async_remote_copy(
            src_ref=o_all.at[head, token_rows(peer), :],
            dst_ref=out.at[:, head_columns(z, head)],
            send_sem=send_o.at[head, peer],
            recv_sem=recv_o.at[head, z],
            device_id={"seq": peer},
            device_id_type=MESH,
        )

    def result_arrival(head, peer):
        return pltpu.make_async_remote_copy(
            src_ref=o_all.at[head, token_rows(peer), :],
            dst_ref=out.at[:, head_columns(peer, head)],
            send_sem=send_o.at[head, peer],
            recv_sem=recv_o.at[head, peer],
            device_id={"seq": peer},
            device_id_type=MESH,
        )

    def own_result(head):
        return pltpu.make_async_copy(
            o_all.at[head, token_rows(z), :],
            out.at[:, head_columns(z, head)],
            recv_o.at[head, z],
        )

    def over_peers(action):
        def step(offset, carry):
            action(lax.rem(z + offset, n))
            return carry

        lax.fori_loop(1, n, step, 0)

    def loop(low, high, action):
        def step(index, carry):
            action(index)
            return carry

        lax.fori_loop(low, high, step, 0)

    def issue(head):
        for which in range(3):
            over_peers(lambda peer: seq_send(which, head, peer).start())
            own_piece(which, head).start()

    def arrive(which, head):
        own_piece(which, head).wait()
        over_peers(lambda peer: seq_arrival(which, head, peer).wait_recv())

    tile = math.gcd(length, 256)

    def attend(head):
        def one_tile(index):
            piece = pl.ds(pl.multiple_of(index * tile, tile), tile)
            query = q_all[head, piece, :]

            def one_span(origin, state):
                top, total, accum = state
                scores = lax.dot_general(
                    query,
                    k_all[origin, head],
                    (((1,), (1,)), ((), ())),
                    preferred_element_type=jnp.float32,
                )
                new_top = jnp.maximum(top, jnp.max(scores, axis=-1, keepdims=True))
                expo = jnp.exp2((scores - new_top) * coef)
                shrink = jnp.exp2((top - new_top) * coef)
                total = total * shrink + jnp.sum(expo, axis=-1, keepdims=True)
                mixed = jnp.dot(
                    expo.astype(jnp.bfloat16),
                    v_all[origin, head],
                    preferred_element_type=jnp.float32,
                )
                return new_top, total, accum * shrink + mixed

            init = (
                jnp.full((tile, 1), -1e30, jnp.float32),
                jnp.zeros((tile, 1), jnp.float32),
                jnp.zeros((tile, HD), jnp.float32),
            )
            _, total, accum = lax.fori_loop(0, span + 1, one_span, init)
            attn = (accum / total).astype(jnp.bfloat16).astype(jnp.float32)
            o_all[head, piece, :] = (attn * gate[head]).astype(jnp.bfloat16)

        loop(0, length // tile, one_tile)

    loop(0, min(AHEAD, heads), issue)

    def one_head(head):
        @pl.when(head + AHEAD < heads)
        def _():
            issue(head + AHEAD)

        for which in range(2):
            arrive(which, head)
            loop(chip + 1, chips, lambda other: chip_send(which, head, other).start())
            if cores == 2:

                @pl.when(core == 0)
                def _():
                    sibling_send(which, head, span).start()

        def from_chip(other):
            origin = other * cores + core
            for which in range(2):
                span_copy(which, head, origin, sibling, send_c.at[which, head, origin]).wait_recv()
                if cores == 2:
                    sibling_send(which, head, origin).start()

        loop(0, chip, from_chip)
        if cores == 2:

            def from_sibling(origin):
                for which in range(2):
                    sibling_send(which, head, origin).wait_recv()

            loop(0, chip, lambda other: from_sibling(other * cores + (1 - core)))

            @pl.when(core == 1)
            def _():
                from_sibling(sibling)

        arrive(2, head)
        attend(head)
        over_peers(lambda peer: result_send(head, peer).start())
        own_result(head).start()

    loop(0, heads, one_head)

    def finish(head):
        for which in range(3):
            over_peers(lambda peer: seq_send(which, head, peer).wait_send())
        for which in range(2):
            loop(chip + 1, chips, lambda other: chip_send(which, head, other).wait_send())
            if cores == 2:
                loop(0, chip, lambda other: sibling_send(which, head, other * cores + core).wait_send())

                @pl.when(core == 0)
                def _():
                    sibling_send(which, head, span).wait_send()

        over_peers(lambda peer: result_send(head, peer).wait_send())
        own_result(head).wait()
        over_peers(lambda peer: result_arrival(head, peer).wait_recv())

    loop(0, heads, finish)


def local(n, spans, q_in, k_in, v_in, timesteps, gate_table):
    _, rows, columns = q_in.shape
    length = rows * n
    heads = columns // HD // n
    chips = spans // 2 if spans % 2 == 0 else spans
    step = lax.dynamic_index_in_dim(timesteps, lax.axis_index("span"), 0, keepdims=False)
    gate = lax.dynamic_slice(
        gate_table, (step, lax.axis_index("seq") * heads * HD), (1, heads * HD)
    ).reshape(heads, 1, HD)
    anywhere = pl.BlockSpec(memory_space=pl.ANY)
    return pl.pallas_call(
        functools.partial(kernel, n, spans),
        out_shape=jax.ShapeDtypeStruct((rows, columns), jnp.bfloat16),
        in_specs=[anywhere] * 3 + [pl.BlockSpec(memory_space=pltpu.VMEM)],
        out_specs=anywhere,
        scratch_shapes=[
            pltpu.VMEM((heads, length, HD), jnp.bfloat16),
            pltpu.VMEM((spans, heads, length, HD), jnp.bfloat16),
            pltpu.VMEM((spans, heads, length, HD), jnp.bfloat16),
            pltpu.VMEM((heads, length, HD), jnp.bfloat16),
            pltpu.SemaphoreType.DMA((3, heads, n)),
            pltpu.SemaphoreType.DMA((3, heads, n)),
            pltpu.SemaphoreType.DMA((2, heads, chips)),
            pltpu.SemaphoreType.DMA((2, heads, spans)),
            pltpu.SemaphoreType.DMA((2, heads, spans)),
            pltpu.SemaphoreType.DMA((heads, n)),
            pltpu.SemaphoreType.DMA((heads, n)),
        ],
        compiler_params=pltpu.CompilerParams(
            collective_id=0, has_side_effects=True, vmem_limit_bytes=48 * 1024 * 1024
        ),
        cost_estimate=pl.CostEstimate(
            flops=4 * heads * length * length * spans * HD,
            bytes_accessed=8 * rows * columns,
            transcendentals=heads * length * length * spans,
        ),
    )(q_in[0], k_in[0], v_in[0], gate)[None]


def solution(mesh):
    in_specs = (
        P(("parts", "span"), "seq", None),
        P(("parts", "span"), "seq", None),
        P(("parts", "span"), "seq", None),
        P("parts"),
        P(),
    )
    out_specs = P(("parts", "span"), "seq", None)
    body = functools.partial(local, mesh.shape["seq"], mesh.shape["span"])
    return jax.shard_map(body, mesh=mesh, in_specs=in_specs, out_specs=out_specs, check_vma=False)
```

```python
import functools
import math

import jax
import jax.numpy as jnp
from jax import lax
from jax.experimental import pallas as pl
from jax.experimental.pallas import tpu as pltpu
from jax.sharding import PartitionSpec as P

HD = 128
AHEAD = 8
MESH = pl.DeviceIdType.MESH


def kernel(
    n, spans, q_in, k_in, v_in, timesteps, gate_table, out, q_all, k_all, v_all, o_all, gates, gate_sem,
    send_z, recv_z, send_x, send_c, recv_s, send_o, recv_o,
):
    heads, length, _ = q_all.shape
    rows = length // n
    cores = 2 if spans % 2 == 0 else 1
    chips = spans // cores
    z = lax.axis_index("seq")
    span = lax.axis_index("span")
    chip = span // cores
    core = lax.rem(span, cores)
    sibling = chip * cores + (cores - 1 - core)
    coef = HD ** (-0.5) * math.log2(math.e)

    barrier = pltpu.get_barrier_semaphore()

    def greet_seq(step, carry):
        pl.semaphore_signal(
            barrier, inc=1, device_id={"seq": lax.rem(z + step, n)}, device_id_type=MESH
        )
        return carry

    def greet_span(step, carry):
        other = lax.rem(chip + step, chips) * cores + core
        pl.semaphore_signal(barrier, inc=1, device_id={"span": other}, device_id_type=MESH)
        return carry

    lax.fori_loop(1, n, greet_seq, 0)
    lax.fori_loop(1, chips, greet_span, 0)
    if cores == 2:
        pl.semaphore_signal(barrier, inc=1, device_id={"span": sibling}, device_id_type=MESH)
    pl.semaphore_wait(barrier, (n - 1) + (chips - 1) + (cores - 1))

    def token_rows(index):
        return pl.ds(pl.multiple_of(index * rows, rows), rows)

    def head_columns(owner, head):
        return pl.ds(pl.multiple_of((owner * heads + head) * HD, HD), HD)

    sources = (k_in, v_in, q_in)

    def landing(which, head, piece):
        if which == 2:
            return q_all.at[head, token_rows(piece), :]
        return (k_all, v_all)[which].at[span, head, token_rows(piece), :]

    def own_piece(which, head):
        return pltpu.make_async_copy(
            sources[which].at[:, head_columns(z, head)],
            landing(which, head, z),
            recv_z.at[which, head, z],
        )

    def seq_send(which, head, peer):
        return pltpu.make_async_remote_copy(
            src_ref=sources[which].at[:, head_columns(peer, head)],
            dst_ref=landing(which, head, z),
            send_sem=send_z.at[which, head, peer],
            recv_sem=recv_z.at[which, head, z],
            device_id={"seq": peer},
            device_id_type=MESH,
        )

    def seq_arrival(which, head, peer):
        return pltpu.make_async_remote_copy(
            src_ref=sources[which].at[:, head_columns(peer, head)],
            dst_ref=landing(which, head, peer),
            send_sem=send_z.at[which, head, peer],
            recv_sem=recv_z.at[which, head, peer],
            device_id={"seq": peer},
            device_id_type=MESH,
        )

    def span_copy(which, head, origin, target, send_sem):
        block = (k_all, v_all)[which].at[origin, head]
        return pltpu.make_async_remote_copy(
            src_ref=block,
            dst_ref=block,
            send_sem=send_sem,
            recv_sem=recv_s.at[which, head, origin],
            device_id={"span": target},
            device_id_type=MESH,
        )

    def chip_send(which, head, other_chip):
        return span_copy(
            which, head, span, other_chip * cores + core, send_x.at[which, head, other_chip]
        )

    def sibling_send(which, head, origin):
        return span_copy(which, head, origin, sibling, send_c.at[which, head, origin])

    def result_send(head, peer):
        return pltpu.make_async_remote_copy(
            src_ref=o_all.at[head, token_rows(peer), :],
            dst_ref=out.at[:, head_columns(z, head)],
            send_sem=send_o.at[head, peer],
            recv_sem=recv_o.at[head, z],
            device_id={"seq": peer},
            device_id_type=MESH,
        )

    def result_arrival(head, peer):
        return pltpu.make_async_remote_copy(
            src_ref=o_all.at[head, token_rows(peer), :],
            dst_ref=out.at[:, head_columns(peer, head)],
            send_sem=send_o.at[head, peer],
            recv_sem=recv_o.at[head, peer],
            device_id={"seq": peer},
            device_id_type=MESH,
        )

    def own_result(head):
        return pltpu.make_async_copy(
            o_all.at[head, token_rows(z), :],
            out.at[:, head_columns(z, head)],
            recv_o.at[head, z],
        )

    def over_peers(action):
        half = n // 2
        side = z // half
        place = lax.rem(z, half)

        def across(offset, carry):
            action((1 - side) * half + lax.rem(place + offset, half))
            return carry

        def beside(offset, carry):
            action(side * half + lax.rem(place + offset, half))
            return carry

        lax.fori_loop(0, half, across, 0)
        lax.fori_loop(1, half, beside, 0)

    def loop(low, high, action):
        def step(index, carry):
            action(index)
            return carry

        lax.fori_loop(low, high, step, 0)

    def issue(head):
        for which in range(3):
            over_peers(lambda peer: seq_send(which, head, peer).start())
            own_piece(which, head).start()

    def arrive(which, head):
        own_piece(which, head).wait()
        over_peers(lambda peer: seq_arrival(which, head, peer).wait_recv())

    tile = math.gcd(length, 256)

    def attend(head):
        table = gates[:, pl.ds(pl.multiple_of(head * HD, HD), HD)]
        chosen = lax.broadcasted_iota(jnp.int32, table.shape, 0) == timesteps[span]
        gate = jnp.sum(jnp.where(chosen, table, 0.0), axis=0, keepdims=True)

        def one_tile(index):
            piece = pl.ds(pl.multiple_of(index * tile, tile), tile)
            query = q_all[head, piece, :]

            def one_span(origin, state):
                top, total, accum = state
                scores = lax.dot_general(
                    query,
                    k_all[origin, head],
                    (((1,), (1,)), ((), ())),
                    preferred_element_type=jnp.float32,
                )
                new_top = jnp.maximum(top, jnp.max(scores, axis=-1, keepdims=True))
                expo = jnp.exp2((scores - new_top) * coef)
                shrink = jnp.exp2((top - new_top) * coef)
                total = total * shrink + jnp.sum(expo, axis=-1, keepdims=True)
                mixed = jnp.dot(
                    expo.astype(jnp.bfloat16),
                    v_all[origin, head],
                    preferred_element_type=jnp.float32,
                )
                return new_top, total, accum * shrink + mixed

            init = (
                jnp.full((tile, 1), -1e30, jnp.float32),
                jnp.zeros((tile, 1), jnp.float32),
                jnp.zeros((tile, HD), jnp.float32),
            )
            _, total, accum = lax.fori_loop(0, span + 1, one_span, init)
            attn = (accum / total).astype(jnp.bfloat16).astype(jnp.float32)
            o_all[head, piece, :] = (attn * gate).astype(jnp.bfloat16)

        loop(0, length // tile, one_tile)

    loop(0, min(AHEAD, heads), issue)
    width = heads * HD
    gate_copy = pltpu.make_async_copy(
        gate_table.at[:, pl.ds(pl.multiple_of(z * width, width), width)], gates, gate_sem
    )
    gate_copy.start()

    def one_head(head):
        @pl.when(head + AHEAD < heads)
        def _():
            issue(head + AHEAD)

        for which in range(2):
            arrive(which, head)
            loop(chip + 1, chips, lambda other: chip_send(which, head, other).start())
            if cores == 2:

                @pl.when(core == 0)
                def _():
                    sibling_send(which, head, span).start()

        def from_chip(other):
            origin = other * cores + core
            for which in range(2):
                span_copy(which, head, origin, sibling, send_c.at[which, head, origin]).wait_recv()
                if cores == 2:
                    sibling_send(which, head, origin).start()

        loop(0, chip, from_chip)
        if cores == 2:

            def from_sibling(origin):
                for which in range(2):
                    sibling_send(which, head, origin).wait_recv()

            loop(0, chip, lambda other: from_sibling(other * cores + (1 - core)))

            @pl.when(core == 1)
            def _():
                from_sibling(sibling)

        arrive(2, head)
        attend(head)
        over_peers(lambda peer: result_send(head, peer).start())
        own_result(head).start()

    gate_copy.wait()
    loop(0, heads, one_head)

    def finish(head):
        for which in range(3):
            over_peers(lambda peer: seq_send(which, head, peer).wait_send())
        for which in range(2):
            loop(chip + 1, chips, lambda other: chip_send(which, head, other).wait_send())
            if cores == 2:
                loop(0, chip, lambda other: sibling_send(which, head, other * cores + core).wait_send())

                @pl.when(core == 0)
                def _():
                    sibling_send(which, head, span).wait_send()

        over_peers(lambda peer: result_send(head, peer).wait_send())
        own_result(head).wait()
        over_peers(lambda peer: result_arrival(head, peer).wait_recv())

    loop(0, heads, finish)


def local(n, spans, q_in, k_in, v_in, timesteps, gate_table):
    _, rows, columns = q_in.shape
    length = rows * n
    heads = columns // HD // n
    chips = spans // 2 if spans % 2 == 0 else spans
    anywhere = pl.BlockSpec(memory_space=pl.ANY)
    return pl.pallas_call(
        functools.partial(kernel, n, spans),
        out_shape=jax.ShapeDtypeStruct((rows, columns), jnp.bfloat16),
        in_specs=[anywhere] * 3 + [pl.BlockSpec(memory_space=pltpu.SMEM), anywhere],
        out_specs=anywhere,
        scratch_shapes=[
            pltpu.VMEM((heads, length, HD), jnp.bfloat16),
            pltpu.VMEM((spans, heads, length, HD), jnp.bfloat16),
            pltpu.VMEM((spans, heads, length, HD), jnp.bfloat16),
            pltpu.VMEM((heads, length, HD), jnp.bfloat16),
            pltpu.VMEM((gate_table.shape[0], heads * HD), jnp.float32),
            pltpu.SemaphoreType.DMA,
            pltpu.SemaphoreType.DMA((3, heads, n)),
            pltpu.SemaphoreType.DMA((3, heads, n)),
            pltpu.SemaphoreType.DMA((2, heads, chips)),
            pltpu.SemaphoreType.DMA((2, heads, spans)),
            pltpu.SemaphoreType.DMA((2, heads, spans)),
            pltpu.SemaphoreType.DMA((heads, n)),
            pltpu.SemaphoreType.DMA((heads, n)),
        ],
        compiler_params=pltpu.CompilerParams(
            collective_id=0, has_side_effects=True, vmem_limit_bytes=61 * 1024 * 1024
        ),
        cost_estimate=pl.CostEstimate(
            flops=4 * heads * length * length * spans * HD,
            bytes_accessed=8 * rows * columns,
            transcendentals=heads * length * length * spans,
        ),
    )(q_in[0], k_in[0], v_in[0], timesteps, gate_table)[None]


def solution(mesh):
    in_specs = (
        P(("parts", "span"), "seq", None),
        P(("parts", "span"), "seq", None),
        P(("parts", "span"), "seq", None),
        P("parts"),
        P(),
    )
    out_specs = P(("parts", "span"), "seq", None)
    body = functools.partial(local, mesh.shape["seq"], mesh.shape["span"])
    return jax.shard_map(body, mesh=mesh, in_specs=in_specs, out_specs=out_specs, check_vma=False)
```

```python
import functools
import math

import jax
import jax.numpy as jnp
from jax import lax
from jax.experimental import pallas as pl
from jax.experimental.pallas import tpu as pltpu
from jax.sharding import PartitionSpec as P

HD = 128
AHEAD = 8
MESH = pl.DeviceIdType.MESH


def kernel(
    n, spans, q_in, k_in, v_in, timesteps, gate_table, out, q_all, k_all, v_all, o_all, gates, gate_sem,
    send_z, recv_z, send_x, send_c, recv_s, send_o, recv_o,
):
    heads, length, _ = q_all.shape
    rows = length // n
    cores = 2 if spans % 2 == 0 else 1
    chips = spans // cores
    z = lax.axis_index("seq")
    span = lax.axis_index("span")
    chip = span // cores
    core = lax.rem(span, cores)
    sibling = chip * cores + (cores - 1 - core)
    coef = HD ** (-0.5) * math.log2(math.e)

    barrier = pltpu.get_barrier_semaphore()

    def greet_seq(step, carry):
        pl.semaphore_signal(
            barrier, inc=1, device_id={"seq": lax.rem(z + step, n)}, device_id_type=MESH
        )
        return carry

    def greet_span(step, carry):
        other = lax.rem(chip + step, chips) * cores + core
        pl.semaphore_signal(barrier, inc=1, device_id={"span": other}, device_id_type=MESH)
        return carry

    lax.fori_loop(1, n, greet_seq, 0)
    lax.fori_loop(1, chips, greet_span, 0)
    if cores == 2:
        pl.semaphore_signal(barrier, inc=1, device_id={"span": sibling}, device_id_type=MESH)
    pl.semaphore_wait(barrier, (n - 1) + (chips - 1) + (cores - 1))

    def token_rows(index):
        return pl.ds(pl.multiple_of(index * rows, rows), rows)

    def head_columns(owner, head):
        return pl.ds(pl.multiple_of((owner * heads + head) * HD, HD), HD)

    sources = (k_in, v_in, q_in)

    def landing(which, head, piece):
        if which == 2:
            return q_all.at[head, token_rows(piece), :]
        return (k_all, v_all)[which].at[span, head, token_rows(piece), :]

    def own_piece(which, head):
        return pltpu.make_async_copy(
            sources[which].at[:, head_columns(z, head)],
            landing(which, head, z),
            recv_z.at[which, head, z],
        )

    def seq_send(which, head, peer):
        return pltpu.make_async_remote_copy(
            src_ref=sources[which].at[:, head_columns(peer, head)],
            dst_ref=landing(which, head, z),
            send_sem=send_z.at[which, head, peer],
            recv_sem=recv_z.at[which, head, z],
            device_id={"seq": peer},
            device_id_type=MESH,
        )

    def seq_arrival(which, head, peer):
        return pltpu.make_async_remote_copy(
            src_ref=sources[which].at[:, head_columns(peer, head)],
            dst_ref=landing(which, head, peer),
            send_sem=send_z.at[which, head, peer],
            recv_sem=recv_z.at[which, head, peer],
            device_id={"seq": peer},
            device_id_type=MESH,
        )

    def span_copy(which, head, origin, target, send_sem):
        block = (k_all, v_all)[which].at[origin, head]
        return pltpu.make_async_remote_copy(
            src_ref=block,
            dst_ref=block,
            send_sem=send_sem,
            recv_sem=recv_s.at[which, head, origin],
            device_id={"span": target},
            device_id_type=MESH,
        )

    def chip_send(which, head, other_chip):
        return span_copy(
            which, head, span, other_chip * cores + core, send_x.at[which, head, other_chip]
        )

    def sibling_send(which, head, origin):
        return span_copy(which, head, origin, sibling, send_c.at[which, head, origin])

    def result_send(head, peer):
        return pltpu.make_async_remote_copy(
            src_ref=o_all.at[head, token_rows(peer), :],
            dst_ref=out.at[:, head_columns(z, head)],
            send_sem=send_o.at[head, peer],
            recv_sem=recv_o.at[head, z],
            device_id={"seq": peer},
            device_id_type=MESH,
        )

    def result_arrival(head, peer):
        return pltpu.make_async_remote_copy(
            src_ref=o_all.at[head, token_rows(peer), :],
            dst_ref=out.at[:, head_columns(peer, head)],
            send_sem=send_o.at[head, peer],
            recv_sem=recv_o.at[head, peer],
            device_id={"seq": peer},
            device_id_type=MESH,
        )

    def own_result(head):
        return pltpu.make_async_copy(
            o_all.at[head, token_rows(z), :],
            out.at[:, head_columns(z, head)],
            recv_o.at[head, z],
        )

    def over_peers(action, part=2):
        half = n // 2
        side = z // half
        place = lax.rem(z, half)

        def across(offset, carry):
            action((1 - side) * half + lax.rem(place + offset, half))
            return carry

        def beside(offset, carry):
            action(side * half + lax.rem(place + offset, half))
            return carry

        if part != 1:
            lax.fori_loop(0, half, across, 0)
        if part != 0:
            lax.fori_loop(1, half, beside, 0)

    def loop(low, high, action):
        def step(index, carry):
            action(index)
            return carry

        lax.fori_loop(low, high, step, 0)

    def issue(head):
        for part in range(2):
            for which in range(3):
                over_peers(lambda peer: seq_send(which, head, peer).start(), part)
        for which in range(3):
            own_piece(which, head).start()

    def arrive(which, head):
        own_piece(which, head).wait()
        over_peers(lambda peer: seq_arrival(which, head, peer).wait_recv())

    tile = math.gcd(length, 256)

    def attend(head):
        table = gates[:, pl.ds(pl.multiple_of(head * HD, HD), HD)]
        chosen = lax.broadcasted_iota(jnp.int32, table.shape, 0) == timesteps[span]
        gate = jnp.sum(jnp.where(chosen, table, 0.0), axis=0, keepdims=True)

        def one_tile(index):
            piece = pl.ds(pl.multiple_of(index * tile, tile), tile)
            query = q_all[head, piece, :]

            def one_span(origin, state):
                top, total, accum = state
                scores = lax.dot_general(
                    query,
                    k_all[origin, head],
                    (((1,), (1,)), ((), ())),
                    preferred_element_type=jnp.float32,
                )
                new_top = jnp.maximum(top, jnp.max(scores, axis=-1, keepdims=True))
                expo = jnp.exp2((scores - new_top) * coef)
                shrink = jnp.exp2((top - new_top) * coef)
                total = total * shrink + jnp.sum(expo, axis=-1, keepdims=True)
                mixed = jnp.dot(
                    expo.astype(jnp.bfloat16),
                    v_all[origin, head],
                    preferred_element_type=jnp.float32,
                )
                return new_top, total, accum * shrink + mixed

            init = (
                jnp.full((tile, 1), -1e30, jnp.float32),
                jnp.zeros((tile, 1), jnp.float32),
                jnp.zeros((tile, HD), jnp.float32),
            )
            _, total, accum = lax.fori_loop(0, span + 1, one_span, init)
            attn = (accum / total).astype(jnp.bfloat16).astype(jnp.float32)
            o_all[head, piece, :] = (attn * gate).astype(jnp.bfloat16)

        loop(0, length // tile, one_tile)

    loop(0, min(AHEAD, heads), issue)
    width = heads * HD
    gate_copy = pltpu.make_async_copy(
        gate_table.at[:, pl.ds(pl.multiple_of(z * width, width), width)], gates, gate_sem
    )
    gate_copy.start()

    def one_head(head):
        @pl.when(head + AHEAD < heads)
        def _():
            issue(head + AHEAD)

        for which in range(2):
            arrive(which, head)
            loop(chip + 1, chips, lambda other: chip_send(which, head, other).start())
            if cores == 2:

                @pl.when(core == 0)
                def _():
                    sibling_send(which, head, span).start()

        def from_chip(other):
            origin = other * cores + core
            for which in range(2):
                span_copy(which, head, origin, sibling, send_c.at[which, head, origin]).wait_recv()
                if cores == 2:
                    sibling_send(which, head, origin).start()

        loop(0, chip, from_chip)
        if cores == 2:

            def from_sibling(origin):
                for which in range(2):
                    sibling_send(which, head, origin).wait_recv()

            loop(0, chip, lambda other: from_sibling(other * cores + (1 - core)))

            @pl.when(core == 1)
            def _():
                from_sibling(sibling)

        arrive(2, head)
        attend(head)
        over_peers(lambda peer: result_send(head, peer).start())
        own_result(head).start()

    gate_copy.wait()
    loop(0, heads, one_head)

    def finish(head):
        for which in range(3):
            over_peers(lambda peer: seq_send(which, head, peer).wait_send())
        for which in range(2):
            loop(chip + 1, chips, lambda other: chip_send(which, head, other).wait_send())
            if cores == 2:
                loop(0, chip, lambda other: sibling_send(which, head, other * cores + core).wait_send())

                @pl.when(core == 0)
                def _():
                    sibling_send(which, head, span).wait_send()

        over_peers(lambda peer: result_send(head, peer).wait_send())
        own_result(head).wait()
        over_peers(lambda peer: result_arrival(head, peer).wait_recv())

    loop(0, heads, finish)


def local(n, spans, q_in, k_in, v_in, timesteps, gate_table):
    _, rows, columns = q_in.shape
    length = rows * n
    heads = columns // HD // n
    chips = spans // 2 if spans % 2 == 0 else spans
    anywhere = pl.BlockSpec(memory_space=pl.ANY)
    return pl.pallas_call(
        functools.partial(kernel, n, spans),
        out_shape=jax.ShapeDtypeStruct((rows, columns), jnp.bfloat16),
        in_specs=[anywhere] * 3 + [pl.BlockSpec(memory_space=pltpu.SMEM), anywhere],
        out_specs=anywhere,
        scratch_shapes=[
            pltpu.VMEM((heads, length, HD), jnp.bfloat16),
            pltpu.VMEM((spans, heads, length, HD), jnp.bfloat16),
            pltpu.VMEM((spans, heads, length, HD), jnp.bfloat16),
            pltpu.VMEM((heads, length, HD), jnp.bfloat16),
            pltpu.VMEM((gate_table.shape[0], heads * HD), jnp.float32),
            pltpu.SemaphoreType.DMA,
            pltpu.SemaphoreType.DMA((3, heads, n)),
            pltpu.SemaphoreType.DMA((3, heads, n)),
            pltpu.SemaphoreType.DMA((2, heads, chips)),
            pltpu.SemaphoreType.DMA((2, heads, spans)),
            pltpu.SemaphoreType.DMA((2, heads, spans)),
            pltpu.SemaphoreType.DMA((heads, n)),
            pltpu.SemaphoreType.DMA((heads, n)),
        ],
        compiler_params=pltpu.CompilerParams(
            collective_id=0, has_side_effects=True, vmem_limit_bytes=59 * 1024 * 1024
        ),
        cost_estimate=pl.CostEstimate(
            flops=4 * heads * length * length * spans * HD,
            bytes_accessed=8 * rows * columns,
            transcendentals=heads * length * length * spans,
        ),
    )(q_in[0], k_in[0], v_in[0], timesteps, gate_table)[None]


def solution(mesh):
    in_specs = (
        P(("parts", "span"), "seq", None),
        P(("parts", "span"), "seq", None),
        P(("parts", "span"), "seq", None),
        P("parts"),
        P(),
    )
    out_specs = P(("parts", "span"), "seq", None)
    body = functools.partial(local, mesh.shape["seq"], mesh.shape["span"])
    return jax.shard_map(body, mesh=mesh, in_specs=in_specs, out_specs=out_specs, check_vma=False)
```

```python
import functools
import math

import jax
import jax.numpy as jnp
from jax import lax
from jax.experimental import pallas as pl
from jax.experimental.pallas import tpu as pltpu
from jax.sharding import PartitionSpec as P

HD = 128
AHEAD = 8
MESH = pl.DeviceIdType.MESH


def kernel(
    n, spans, q_in, k_in, v_in, timesteps, gate_table, out, q_all, k_all, v_all, o_all, gates, gate_sem,
    send_z, recv_z, send_x, send_c, recv_s, send_o, recv_o,
):
    heads, length, _ = q_all.shape
    rows = length // n
    cores = 2 if spans % 2 == 0 else 1
    chips = spans // cores
    z = lax.axis_index("seq")
    span = lax.axis_index("span")
    chip = span // cores
    core = lax.rem(span, cores)
    sibling = chip * cores + (cores - 1 - core)
    coef = HD ** (-0.5) * math.log2(math.e)

    barrier = pltpu.get_barrier_semaphore()

    def greet_seq(step, carry):
        pl.semaphore_signal(
            barrier, inc=1, device_id={"seq": lax.rem(z + step, n)}, device_id_type=MESH
        )
        return carry

    def greet_span(step, carry):
        other = lax.rem(chip + step, chips) * cores + core
        pl.semaphore_signal(barrier, inc=1, device_id={"span": other}, device_id_type=MESH)
        return carry

    lax.fori_loop(1, n, greet_seq, 0)
    lax.fori_loop(1, chips, greet_span, 0)
    if cores == 2:
        pl.semaphore_signal(barrier, inc=1, device_id={"span": sibling}, device_id_type=MESH)
    pl.semaphore_wait(barrier, (n - 1) + (chips - 1) + (cores - 1))

    def token_rows(index):
        return pl.ds(pl.multiple_of(index * rows, rows), rows)

    def head_columns(owner, head):
        return pl.ds(pl.multiple_of((owner * heads + head) * HD, HD), HD)

    sources = (k_in, v_in, q_in)

    def landing(which, head, piece):
        if which == 2:
            return q_all.at[head, token_rows(piece), :]
        return (k_all, v_all)[which].at[span, head, token_rows(piece), :]

    def own_piece(which, head):
        return pltpu.make_async_copy(
            sources[which].at[:, head_columns(z, head)],
            landing(which, head, z),
            recv_z.at[which, head, z],
        )

    def seq_send(which, head, peer):
        return pltpu.make_async_remote_copy(
            src_ref=sources[which].at[:, head_columns(peer, head)],
            dst_ref=landing(which, head, z),
            send_sem=send_z.at[which, head, peer],
            recv_sem=recv_z.at[which, head, z],
            device_id={"seq": peer},
            device_id_type=MESH,
        )

    def seq_arrival(which, head, peer):
        return pltpu.make_async_remote_copy(
            src_ref=sources[which].at[:, head_columns(peer, head)],
            dst_ref=landing(which, head, peer),
            send_sem=send_z.at[which, head, peer],
            recv_sem=recv_z.at[which, head, peer],
            device_id={"seq": peer},
            device_id_type=MESH,
        )

    def span_copy(which, head, origin, target, send_sem):
        block = (k_all, v_all)[which].at[origin, head]
        return pltpu.make_async_remote_copy(
            src_ref=block,
            dst_ref=block,
            send_sem=send_sem,
            recv_sem=recv_s.at[which, head, origin],
            device_id={"span": target},
            device_id_type=MESH,
        )

    def chip_send(which, head, other_chip):
        return span_copy(
            which, head, span, other_chip * cores + core, send_x.at[which, head, other_chip]
        )

    def sibling_send(which, head, origin):
        return span_copy(which, head, origin, sibling, send_c.at[which, head, origin])

    def result_send(head, peer):
        return pltpu.make_async_remote_copy(
            src_ref=o_all.at[head, token_rows(peer), :],
            dst_ref=out.at[:, head_columns(z, head)],
            send_sem=send_o.at[head, peer],
            recv_sem=recv_o.at[head, z],
            device_id={"seq": peer},
            device_id_type=MESH,
        )

    def result_arrival(head, peer):
        return pltpu.make_async_remote_copy(
            src_ref=o_all.at[head, token_rows(peer), :],
            dst_ref=out.at[:, head_columns(peer, head)],
            send_sem=send_o.at[head, peer],
            recv_sem=recv_o.at[head, peer],
            device_id={"seq": peer},
            device_id_type=MESH,
        )

    def own_result(head):
        return pltpu.make_async_copy(
            o_all.at[head, token_rows(z), :],
            out.at[:, head_columns(z, head)],
            recv_o.at[head, z],
        )

    def over_peers(action, part=2):
        half = n // 2
        side = z // half
        place = lax.rem(z, half)

        def across(offset, carry):
            action((1 - side) * half + lax.rem(place + offset, half))
            return carry

        def beside(offset, carry):
            action(side * half + lax.rem(place + offset, half))
            return carry

        if part != 1:
            lax.fori_loop(0, half, across, 0)
        if part != 0:
            lax.fori_loop(1, half, beside, 0)

    def loop(low, high, action):
        def step(index, carry):
            action(index)
            return carry

        lax.fori_loop(low, high, step, 0)

    def issue(head):
        for part in range(2):
            for which in range(3):
                over_peers(lambda peer: seq_send(which, head, peer).start(), part)
        for which in range(3):
            own_piece(which, head).start()

    def arrive(which, head):
        own_piece(which, head).wait()
        over_peers(lambda peer: seq_arrival(which, head, peer).wait_recv())

    owners = math.gcd(n, max(1, 256 // rows))
    tile = rows * owners
    half_tiles = max(1, n // owners // 2)

    def attend(head):
        table = gates[:, pl.ds(pl.multiple_of(head * HD, HD), HD)]
        chosen = lax.broadcasted_iota(jnp.int32, table.shape, 0) == timesteps[span]
        gate = jnp.sum(jnp.where(chosen, table, 0.0), axis=0, keepdims=True)

        def one_tile(step):
            side = (z // owners // half_tiles + 1 + step // half_tiles) % 2
            place = (z // owners + 1 + step) % half_tiles
            index = side * half_tiles + place
            piece = pl.ds(pl.multiple_of(index * tile, tile), tile)
            query = q_all[head, piece, :]

            def one_span(origin, state):
                top, total, accum = state
                scores = lax.dot_general(
                    query,
                    k_all[origin, head],
                    (((1,), (1,)), ((), ())),
                    preferred_element_type=jnp.float32,
                )
                new_top = jnp.maximum(top, jnp.max(scores, axis=-1, keepdims=True))
                expo = jnp.exp2((scores - new_top) * coef)
                shrink = jnp.exp2((top - new_top) * coef)
                total = total * shrink + jnp.sum(expo, axis=-1, keepdims=True)
                mixed = jnp.dot(
                    expo.astype(jnp.bfloat16),
                    v_all[origin, head],
                    preferred_element_type=jnp.float32,
                )
                return new_top, total, accum * shrink + mixed

            init = (
                jnp.full((tile, 1), -1e30, jnp.float32),
                jnp.zeros((tile, 1), jnp.float32),
                jnp.zeros((tile, HD), jnp.float32),
            )
            _, total, accum = lax.fori_loop(0, span + 1, one_span, init)
            attn = (accum / total).astype(jnp.bfloat16).astype(jnp.float32)
            o_all[head, piece, :] = (attn * gate).astype(jnp.bfloat16)

            def give(owner):
                @pl.when(owner != z)
                def _():
                    result_send(head, owner).start()

                @pl.when(owner == z)
                def _():
                    own_result(head).start()

            loop(index * owners, (index + 1) * owners, give)

        loop(0, length // tile, one_tile)

    loop(0, min(AHEAD, heads), issue)
    width = heads * HD
    gate_copy = pltpu.make_async_copy(
        gate_table.at[:, pl.ds(pl.multiple_of(z * width, width), width)], gates, gate_sem
    )
    gate_copy.start()

    def one_head(head):
        @pl.when(head + AHEAD < heads)
        def _():
            issue(head + AHEAD)

        for which in range(2):
            arrive(which, head)
            loop(chip + 1, chips, lambda other: chip_send(which, head, other).start())
            if cores == 2:

                @pl.when(core == 0)
                def _():
                    sibling_send(which, head, span).start()

        def from_chip(other):
            origin = other * cores + core
            for which in range(2):
                span_copy(which, head, origin, sibling, send_c.at[which, head, origin]).wait_recv()
                if cores == 2:
                    sibling_send(which, head, origin).start()

        loop(0, chip, from_chip)
        if cores == 2:

            def from_sibling(origin):
                for which in range(2):
                    sibling_send(which, head, origin).wait_recv()

            loop(0, chip, lambda other: from_sibling(other * cores + (1 - core)))

            @pl.when(core == 1)
            def _():
                from_sibling(sibling)

        arrive(2, head)
        attend(head)

    gate_copy.wait()
    loop(0, heads, one_head)

    def finish(head):
        for which in range(3):
            over_peers(lambda peer: seq_send(which, head, peer).wait_send())
        for which in range(2):
            loop(chip + 1, chips, lambda other: chip_send(which, head, other).wait_send())
            if cores == 2:
                loop(0, chip, lambda other: sibling_send(which, head, other * cores + core).wait_send())

                @pl.when(core == 0)
                def _():
                    sibling_send(which, head, span).wait_send()

        over_peers(lambda peer: result_send(head, peer).wait_send())
        own_result(head).wait()
        over_peers(lambda peer: result_arrival(head, peer).wait_recv())

    loop(0, heads, finish)


def local(n, spans, q_in, k_in, v_in, timesteps, gate_table):
    _, rows, columns = q_in.shape
    length = rows * n
    heads = columns // HD // n
    chips = spans // 2 if spans % 2 == 0 else spans
    anywhere = pl.BlockSpec(memory_space=pl.ANY)
    return pl.pallas_call(
        functools.partial(kernel, n, spans),
        out_shape=jax.ShapeDtypeStruct((rows, columns), jnp.bfloat16),
        in_specs=[anywhere] * 3 + [pl.BlockSpec(memory_space=pltpu.SMEM), anywhere],
        out_specs=anywhere,
        scratch_shapes=[
            pltpu.VMEM((heads, length, HD), jnp.bfloat16),
            pltpu.VMEM((spans, heads, length, HD), jnp.bfloat16),
            pltpu.VMEM((spans, heads, length, HD), jnp.bfloat16),
            pltpu.VMEM((heads, length, HD), jnp.bfloat16),
            pltpu.VMEM((gate_table.shape[0], heads * HD), jnp.float32),
            pltpu.SemaphoreType.DMA,
            pltpu.SemaphoreType.DMA((3, heads, n)),
            pltpu.SemaphoreType.DMA((3, heads, n)),
            pltpu.SemaphoreType.DMA((2, heads, chips)),
            pltpu.SemaphoreType.DMA((2, heads, spans)),
            pltpu.SemaphoreType.DMA((2, heads, spans)),
            pltpu.SemaphoreType.DMA((heads, n)),
            pltpu.SemaphoreType.DMA((heads, n)),
        ],
        compiler_params=pltpu.CompilerParams(
            collective_id=0, has_side_effects=True, vmem_limit_bytes=59 * 1024 * 1024
        ),
        cost_estimate=pl.CostEstimate(
            flops=4 * heads * length * length * spans * HD,
            bytes_accessed=8 * rows * columns,
            transcendentals=heads * length * length * spans,
        ),
    )(q_in[0], k_in[0], v_in[0], timesteps, gate_table)[None]


def solution(mesh):
    in_specs = (
        P(("parts", "span"), "seq", None),
        P(("parts", "span"), "seq", None),
        P(("parts", "span"), "seq", None),
        P("parts"),
        P(),
    )
    out_specs = P(("parts", "span"), "seq", None)
    body = functools.partial(local, mesh.shape["seq"], mesh.shape["span"])
    return jax.shard_map(body, mesh=mesh, in_specs=in_specs, out_specs=out_specs, check_vma=False)
```
